32 devices in a mesh: frame: 16 (over z, y, x), head: 2 (over core).
Axes of the slice: x: 2, y: 2, z: 4, core: 2. Of those that a mesh axis runs over, the one named last changes fastest.
Arguments:
- queries: bfloat16 [4096, 5120], P('frame', 'head'), may hold values from -12 to 12
- keys: bfloat16 [4096, 5120], P('frame', 'head'), may hold values from -12 to 12
- values: bfloat16 [4096, 5120], P('frame', 'head'), may hold values from -6 to 6
- policy_grad: bfloat16 [4096, 5120], P('frame', 'head'), may hold values from -6 to 6
- ref_velocity: bfloat16 [4096, 5120], P('frame', 'head'), may hold values from -6 to 6
- key_lists: int32 [32, 6], P('frame'), may hold values from 0 to 31, as said below
- frame_tokens: int32 [32], replicated, may hold values from 32 to 128, as said below
Outputs:
- grad_queries: bfloat16 [4096, 5120], P('frame', 'head')
- grad_keys: bfloat16 [4096, 5120], P('frame', 'head')
- grad_values: bfloat16 [4096, 5120], P('frame', 'head')
The draws below stay inside these ranges and needn't reach their ends.
Inputs may be any that keep to these rules, and one draw needn't show every extreme that they name: `key_lists`: row b holds 6 distinct blocks: b, the next block of the same index of frame (cyclic over its 2 blocks), and four blocks on indices of frame that differ from b's index by distinct signed powers of two. `frame_tokens`: some block is full.
All inputs are finite; a program needn't handle non-finite values.
Results may differ from the reference program's by a relative error of at most 0.011.
Values may be sent and summed in bfloat16 or wider, within the bound.
A program may use at most 192 MiB of HBM per device.

```python
import math
import jax
import jax.numpy as jnp
from jax import lax

HEADS = 40
HD = 128
BLK = 128
KLIST = 6
TOKENS = 4096
FBLK = 2
NBLK = 32
SHARDS = 16
LEVELS = 4


def draw_queries(key, part):
    shape = (TOKENS, HEADS * HD)
    base = jax.random.normal(jax.random.fold_in(key, 1), shape, jnp.float32)
    return base.astype(jnp.bfloat16)


def draw_keys(key, part):
    shape = (TOKENS, HEADS * HD)
    base = jax.random.normal(jax.random.fold_in(key, 2), shape, jnp.float32)
    return base.astype(jnp.bfloat16)


def draw_frame_tokens(key, part):
    counts = jax.random.randint(jax.random.fold_in(key, 3), (NBLK,), BLK // 4, BLK + 1, jnp.int32)
    counts = counts.at[0].set(BLK)
    return counts.at[1].set(BLK // 4)


def draw_key_lists(key, part):
    blocks = jnp.arange(NBLK, dtype=jnp.int32)
    device = blocks // FBLK
    place = blocks % FBLK
    first = blocks
    second = device * FBLK + (place + 1) % FBLK
    steps = []
    for level in range(LEVELS):
        steps.append(1 << level)
        steps.append(-(1 << level))
    steps = jnp.array(steps, dtype=jnp.int32)
    target = device[:, None] + steps[None, :]
    inside = (target >= 0) & (target < SHARDS)
    scores = jax.random.randint(jax.random.fold_in(key, 4), (NBLK, 2 * LEVELS), 0, 1 << 16, jnp.int32) * 64 + jnp.arange(2 * LEVELS, dtype=jnp.int32)[None, :]
    scores = jnp.where(inside, scores, -1)
    picked = jax.lax.top_k(scores, 4)[1]
    chosen = jnp.take_along_axis(target, picked, axis=1)
    within = jax.random.randint(jax.random.fold_in(key, 5), (NBLK, 4), 0, FBLK, jnp.int32)
    far_blocks = chosen * FBLK + within
    return jnp.concatenate([first[:, None], second[:, None], far_blocks], axis=1).astype(jnp.int32)


def level_of(key, shape, cuts, smallest, largest):
    gain, own = 1.0, jax.random.fold_in(key, 6)
    for dim, blocks in cuts:
        steps = jnp.exp(jax.random.uniform(jax.random.fold_in(own, dim), (blocks,), jnp.float32, smallest / len(cuts), largest / len(cuts)))
        gain = gain * jnp.repeat(steps, shape[dim] // blocks).reshape([-1 if axis == dim else 1 for axis in range(len(shape))])
    return gain


def normal_values(key, extent, width, bound, split=(), kind=jnp.bfloat16):
    result = width * jax.random.normal(key, extent, jnp.float32)
    if split:
        result = result * level_of(key, extent, split, -0.22, 0.18)
    return jnp.clip(result, -bound, bound).astype(kind)


def setup_inputs(seed: int = 0) -> dict:
    splits = jax.random.split(jax.random.key(seed), 8)
    return {
        "queries": draw_queries(jax.random.fold_in(splits[7], 71), 0),
        "keys": draw_keys(jax.random.fold_in(splits[7], 71), 0),
        "values": normal_values(splits[2], (TOKENS, HEADS * HD), 1.0, 6.0, ((0, 16), (1, 2))),
        "policy_grad": normal_values(splits[3], (TOKENS, HEADS * HD), 1.0, 6.0, ((0, 16), (1, 2))),
        "ref_velocity": normal_values(splits[4], (TOKENS, HEADS * HD), 1.0, 6.0, ((0, 16), (1, 2))),
        "key_lists": draw_key_lists(jax.random.fold_in(splits[7], 71), 0),
        "frame_tokens": draw_frame_tokens(jax.random.fold_in(splits[7], 71), 0),
    }


kl_weight = 1.0

def block_forward(query_block, key_block, value_block, valid, scale):
    scores = jnp.einsum('qhd,khd->hqk', query_block.astype(jnp.float32), key_block.astype(jnp.float32), precision=lax.Precision.HIGHEST) * scale
    scores = jnp.where(valid[None, None, :], scores, -1e+30)
    highest = lax.optimization_barrier(jnp.max(scores, axis=-1, keepdims=True))
    expd = jnp.exp(scores - highest)
    probs = expd / lax.optimization_barrier(jnp.sum(expd, axis=-1, keepdims=True))
    probs16 = probs.astype(jnp.bfloat16)
    attn = jnp.einsum('hqk,khd->qhd', probs16.astype(jnp.float32), value_block.astype(jnp.float32), precision=lax.Precision.HIGHEST)
    return (probs, probs16, attn)

def reference(queries, keys, values, policy_grad, ref_velocity, key_lists, frame_tokens):
    scale = 1.0 / math.sqrt(HD)
    query4 = queries.reshape(NBLK, BLK, HEADS, HD)
    key4 = keys.reshape(NBLK, BLK, HEADS, HD)
    value4 = values.reshape(NBLK, BLK, HEADS, HD)

    def fetch(ids):
        key_block = key4[ids].reshape(KLIST * BLK, HEADS, HD)
        value_block = value4[ids].reshape(KLIST * BLK, HEADS, HD)
        valid = (jnp.arange(BLK, dtype=jnp.int32)[None, :] < frame_tokens[ids][:, None]).reshape(-1)
        return (key_block, value_block, valid)

    def forward_one(index):
        key_block, value_block, valid = fetch(key_lists[index])
        return block_forward(query4[index], key_block, value_block, valid, scale)[2]
    attn_all = lax.map(forward_one, jnp.arange(NBLK, dtype=jnp.int32))
    diff = attn_all - ref_velocity.reshape(NBLK, BLK, HEADS, HD).astype(jnp.float32)
    kl = lax.optimization_barrier(jnp.sum(diff * diff, axis=(2, 3))) / (HEADS * HD)
    grad_attn = policy_grad.reshape(NBLK, BLK, HEADS, HD).astype(jnp.float32) + kl_weight * diff / (1.0 + kl)[:, :, None, None]
    grad16 = grad_attn.astype(jnp.bfloat16)

    def backward_one(index):
        key_block, value_block, valid = fetch(key_lists[index])
        probs, probs16, attn = block_forward(query4[index], key_block, value_block, valid, scale)
        upstream = grad16[index].astype(jnp.float32)
        grad_probs = jnp.einsum('qhd,khd->hqk', upstream, value_block.astype(jnp.float32), precision=lax.Precision.HIGHEST)
        delta = lax.optimization_barrier(jnp.sum(upstream * attn, axis=-1)).T
        grad_scores16 = (probs * (grad_probs - delta[:, :, None])).astype(jnp.bfloat16).astype(jnp.float32)
        grad_q = (jnp.einsum('hqk,khd->qhd', grad_scores16, key_block.astype(jnp.float32), precision=lax.Precision.HIGHEST) * scale).astype(jnp.bfloat16)
        part_k = jnp.einsum('hqk,qhd->khd', grad_scores16, query4[index].astype(jnp.float32), precision=lax.Precision.HIGHEST) * scale
        part_v = jnp.einsum('hqk,qhd->khd', probs16.astype(jnp.float32), upstream, precision=lax.Precision.HIGHEST)
        return (grad_q, part_k.reshape(KLIST, BLK * HEADS * HD), part_v.reshape(KLIST, BLK * HEADS * HD))

    def device_step(carry, device):
        acc_k, acc_v = carry
        blocks = device * FBLK + jnp.arange(FBLK, dtype=jnp.int32)
        grad_q, part_k, part_v = lax.map(backward_one, blocks)
        ids = key_lists[blocks].reshape(-1).astype(jnp.int32)
        same = (ids[:, None] == ids[None, :]).astype(jnp.float32)
        earlier = lax.optimization_barrier(jnp.sum(jnp.tril(same, -1), axis=1))
        first = (earlier == 0.0)[:, None]
        remote = (ids // FBLK != device)[:, None]
        part_k = jnp.dot(same, part_k.reshape(FBLK * KLIST, -1), precision=lax.Precision.HIGHEST)
        part_v = jnp.dot(same, part_v.reshape(FBLK * KLIST, -1), precision=lax.Precision.HIGHEST)
        round_k = lax.optimization_barrier(part_k.astype(jnp.bfloat16)).astype(jnp.float32)
        round_v = lax.optimization_barrier(part_v.astype(jnp.bfloat16)).astype(jnp.float32)
        part_k = jnp.where(remote, round_k, part_k)
        part_v = jnp.where(remote, round_v, part_v)
        acc_k = acc_k.at[ids].add(jnp.where(first, part_k, jnp.float32(0.0)))
        acc_v = acc_v.at[ids].add(jnp.where(first, part_v, jnp.float32(0.0)))
        return ((acc_k, acc_v), grad_q)
    zeros = jnp.zeros((NBLK, BLK * HEADS * HD), jnp.float32)
    (acc_k, acc_v), grad_q = lax.scan(device_step, (zeros, zeros), jnp.arange(SHARDS, dtype=jnp.int32))
    grad_queries = grad_q.reshape(TOKENS, HEADS * HD)
    grad_keys = acc_k.reshape(TOKENS, HEADS * HD).astype(jnp.bfloat16)
    grad_values = acc_v.reshape(TOKENS, HEADS * HD).astype(jnp.bfloat16)
    return (grad_queries, grad_keys, grad_values)
```

```python
import functools
import math

import jax
import jax.numpy as jnp
from jax import lax
from jax.experimental import pallas as pl
from jax.experimental.pallas import tpu as pltpu
from jax.sharding import PartitionSpec as P

HD = 128
BLK = 128
KL_WEIGHT = 1.0
VMEM = 40 * 1024 * 1024

NT = (((1,), (1,)), ((), ()))
NN = (((1,), (0,)), ((), ()))
TN = (((0,), (0,)), ((), ()))


def dot(a, b, dims):
    return lax.dot_general(a, b, dims, preferred_element_type=jnp.float32)


def fetch(pool, held, sems, head, slot):
    cols = pl.ds(pl.multiple_of(head * HD, HD), HD)
    return [
        pltpu.make_async_copy(ref.at[:, cols], held.at[slot, n], sems.at[slot, n])
        for n, ref in enumerate(pool)
    ]


def rotate_in(pool, held, sems, head, heads):
    slot = lax.rem(head, 2)

    @pl.when(head == 0)
    def _():
        for copy in fetch(pool, held, sems, head, slot):
            copy.start()

    @pl.when(head + 1 < heads)
    def _():
        for copy in fetch(pool, held, sems, head + 1, 1 - slot):
            copy.start()

    for copy in fetch(pool, held, sems, head, slot):
        copy.wait()
    return slot


def listed(held, slot, where_ref, first, list_len, rows, part):
    out = []
    for n in range(list_len):
        code = where_ref[first + n]
        start = pl.multiple_of(lax.rem(code, rows // BLK) * BLK + part * rows, BLK)
        out.append(held[slot, lax.div(code, rows // BLK), pl.ds(start, BLK), :])
    return jnp.concatenate(out, axis=0)


def forward_kernel(n_pool, blocks, list_len, heads, where_ref, count_ref, q_ref, ref_ref, *rest):
    pool, (attn_ref, probs_ref, sq_ref, held, sems) = rest[:n_pool], rest[n_pool:]
    head = pl.program_id(0)
    rows = blocks * BLK
    slot = rotate_in(pool, held, sems, head, heads)
    scale = 1.0 / math.sqrt(HD)
    lane = lax.broadcasted_iota(jnp.int32, (BLK, BLK), 1)

    @pl.when(head == 0)
    def _():
        sq_ref[...] = jnp.zeros_like(sq_ref)

    for b in range(blocks):
        mine = pl.ds(b * BLK, BLK)
        k = listed(held, slot, where_ref, b * list_len, list_len, rows, 0)
        v = listed(held, slot, where_ref, b * list_len, list_len, rows, 1)
        s = dot(q_ref[mine, :], k, NT) * scale
        s = jnp.concatenate(
            [
                jnp.where(
                    lane < count_ref[b * list_len + n], s[:, n * BLK : (n + 1) * BLK], -1e30
                )
                for n in range(list_len)
            ],
            axis=1,
        )
        e = jnp.exp(s - jnp.max(s, axis=-1, keepdims=True))
        p = e * (1.0 / jnp.sum(e, axis=-1, keepdims=True))
        p16 = p.astype(jnp.bfloat16)
        probs_ref[0, mine, :] = p16
        attn = dot(p16, v, NN)
        attn_ref[mine, :] = attn
        diff = attn - ref_ref[mine, :].astype(jnp.float32)
        sq_ref[mine, :] += diff * diff


def backward_kernel(
    n_pool, blocks, list_len, heads, where_ref, q_ref, pg_ref, ref_ref, attn_ref, probs_ref, inv_ref, *rest
):
    pool, dq_ref, outs = rest[:n_pool], rest[n_pool], rest[n_pool + 1 : 2 * n_pool + 1]
    held, sems, part, out_sems = rest[2 * n_pool + 1 :]
    head = pl.program_id(0)
    rows = blocks * BLK
    slot = rotate_in(pool, held, sems, head, heads)
    scale = 1.0 / math.sqrt(HD)

    def leave(which, at):
        cols = pl.ds(pl.multiple_of(which * HD, HD), HD)
        return [
            pltpu.make_async_copy(part.at[at, n], ref.at[:, cols], out_sems.at[at, n])
            for n, ref in enumerate(outs)
        ]

    @pl.when(head >= 2)
    def _():
        for copy in leave(head - 2, slot):
            copy.wait()

    part[slot] = jnp.zeros(part.shape[1:], part.dtype)
    for b in range(blocks):
        mine = pl.ds(b * BLK, BLK)
        k = listed(held, slot, where_ref, b * list_len, list_len, rows, 0)
        v = listed(held, slot, where_ref, b * list_len, list_len, rows, 1)
        attn = attn_ref[mine, :]
        q = q_ref[mine, :]
        p16 = probs_ref[0, mine, :]
        diff = attn - ref_ref[mine, :].astype(jnp.float32)
        g16 = (pg_ref[mine, :].astype(jnp.float32) + KL_WEIGHT * diff * inv_ref[mine, :]).astype(
            jnp.bfloat16
        )
        delta = jnp.sum(g16.astype(jnp.float32) * attn, axis=-1, keepdims=True)
        ds16 = (p16.astype(jnp.float32) * (dot(g16, v, NT) - delta)).astype(jnp.bfloat16)
        dq_ref[mine, :] = (dot(ds16, k, NN) * scale).astype(jnp.bfloat16)
        dk = dot(ds16, q, TN) * scale
        dv = dot(p16, g16, TN)
        for n in range(list_len):
            code = where_ref[b * list_len + n]
            at, within = lax.div(code, blocks), lax.rem(code, blocks)
            for kind, value in ((0, dk), (1, dv)):
                start = pl.multiple_of(within * BLK + kind * rows, BLK)
                piece = value[n * BLK : (n + 1) * BLK, :]
                if b > 0:
                    piece = piece + part[slot, at, pl.ds(start, BLK), :].astype(jnp.float32)
                part[slot, at, pl.ds(start, BLK), :] = piece.astype(jnp.bfloat16)

    for copy in leave(head, slot):
        copy.start()

    @pl.when(head == heads - 1)
    def _():
        if heads > 1:
            for copy in leave(head - 1, 1 - slot):
                copy.wait()
        for copy in leave(head, slot):
            copy.wait()


def forward(where, counts, queries, ref, pool, first, heads, blocks, list_len):
    rows, keys = blocks * BLK, list_len * BLK
    n_pool = len(pool)
    column = pl.BlockSpec((rows, HD), lambda h, *_: (0, first + h))
    here = pl.BlockSpec((rows, HD), lambda h, *_: (0, h))
    return pl.pallas_call(
        functools.partial(forward_kernel, n_pool, blocks, list_len, heads),
        grid_spec=pltpu.PrefetchScalarGridSpec(
            num_scalar_prefetch=2,
            grid=(heads,),
            in_specs=[column, column] + [pl.BlockSpec(memory_space=pl.ANY)] * n_pool,
            out_specs=[
                here,
                pl.BlockSpec((1, rows, keys), lambda h, *_: (h, 0, 0)),
                pl.BlockSpec((rows, HD), lambda h, *_: (0, 0)),
            ],
            scratch_shapes=[
                pltpu.VMEM((2, n_pool, 2 * rows, HD), jnp.bfloat16),
                pltpu.SemaphoreType.DMA((2, n_pool)),
            ],
        ),
        out_shape=[
            jax.ShapeDtypeStruct((rows, heads * HD), jnp.float32),
            jax.ShapeDtypeStruct((heads, rows, keys), jnp.bfloat16),
            jax.ShapeDtypeStruct((rows, HD), jnp.float32),
        ],
        compiler_params=pltpu.CompilerParams(vmem_limit_bytes=VMEM),
        cost_estimate=pl.CostEstimate(
            flops=4 * heads * rows * keys * HD,
            bytes_accessed=heads * (n_pool * 4 * rows * HD + rows * keys * 2 + rows * HD * 8),
            transcendentals=heads * rows * keys,
        ),
        name="forward",
    )(where, counts, queries, ref, *pool)


def backward(where, queries, policy, ref, attn, probs, inv, pool, first, heads, blocks, list_len):
    rows, keys = blocks * BLK, list_len * BLK
    n_pool = len(pool)
    column = pl.BlockSpec((rows, HD), lambda h, *_: (0, first + h))
    here = pl.BlockSpec((rows, HD), lambda h, *_: (0, h))
    anywhere = pl.BlockSpec(memory_space=pl.ANY)
    return pl.pallas_call(
        functools.partial(backward_kernel, n_pool, blocks, list_len, heads),
        grid_spec=pltpu.PrefetchScalarGridSpec(
            num_scalar_prefetch=1,
            grid=(heads,),
            in_specs=[
                column,
                column,
                column,
                here,
                pl.BlockSpec((1, rows, keys), lambda h, *_: (h, 0, 0)),
                pl.BlockSpec((rows, HD), lambda h, *_: (0, 0)),
            ]
            + [anywhere] * n_pool,
            out_specs=[here] + [anywhere] * n_pool,
            scratch_shapes=[
                pltpu.VMEM((2, n_pool, 2 * rows, HD), jnp.bfloat16),
                pltpu.SemaphoreType.DMA((2, n_pool)),
                pltpu.VMEM((2, n_pool, 2 * rows, HD), jnp.bfloat16),
                pltpu.SemaphoreType.DMA((2, n_pool)),
            ],
        ),
        out_shape=[jax.ShapeDtypeStruct((rows, heads * HD), jnp.bfloat16)]
        + [jax.ShapeDtypeStruct((2 * rows, heads * HD), jnp.bfloat16)] * n_pool,
        compiler_params=pltpu.CompilerParams(vmem_limit_bytes=VMEM),
        cost_estimate=pl.CostEstimate(
            flops=8 * heads * rows * keys * HD,
            bytes_accessed=heads * (n_pool * 8 * rows * HD + rows * keys * 2 + rows * HD * 12),
            transcendentals=0,
        ),
        name="backward",
    )(where, queries, policy, ref, attn, probs, inv, *pool)


def shift(value, steps):
    count = lax.axis_size("frame")
    pairs = [(s, s + steps) for s in range(count) if 0 <= s + steps < count]
    return lax.ppermute(value, "frame", pairs)


def swap(value, bit):
    count = lax.axis_size("frame")
    return lax.ppermute(value, "frame", [(s, s ^ bit) for s in range(count)])


def add(*terms):
    total = terms[0].astype(jnp.float32)
    for term in terms[1:]:
        total = total + term.astype(jnp.float32)
    return total.astype(jnp.bfloat16)


def gather(kv, corner, upper, levels):
    far = [(shift(kv, 4), shift(kv, -4))]
    across, along = swap(kv, 1), swap(kv, 2)
    for level in range(3, levels):
        step = 1 << (level - 1)
        far.append((shift(far[-1][0], step), shift(far[-1][1], -step)))
    cross = swap(jnp.where(upper, far[0][0], far[0][1]), 2)
    diagonal = swap(jnp.where(corner, along, cross), 1)
    return [kv, across, along, cross, diagonal] + [x for pair in far for x in pair]


def scatter(parts, corner, upper, levels):
    own, across, along, cross, diagonal = parts[:5]
    before, after = list(parts[5::2]), list(parts[6::2])
    zero = jnp.zeros((), jnp.bfloat16)
    diagonal = swap(diagonal, 1)
    across = swap(across, 1)
    for level in range(levels - 1, 2, -1):
        step = 1 << (level - 1)
        n = level - 2
        back, forth = shift(before[n], -step), shift(after[n], step)
        if n > 1:
            before[n - 1], after[n - 1] = add(before[n - 1], back), add(after[n - 1], forth)
        else:
            extra = (back, forth)
    cross = swap(add(cross, jnp.where(corner, zero, diagonal)), 2)
    along = swap(add(along, jnp.where(corner, diagonal, zero)), 2)
    more = extra if levels > 3 else (zero, zero)
    first = add(before[0], more[0], jnp.where(upper, cross, zero))
    second = add(after[0], more[1], jnp.where(upper, zero, cross))
    return add(own, across, along, shift(first, -4), shift(second, 4))


def places(gap, me, levels):
    corner_of = me % 4
    upper = corner_of >= 2
    odd = corner_of % 2 == 1
    at = jnp.zeros_like(gap)
    before_1 = jnp.where(odd, 1, 4)
    after_1 = jnp.where(odd, 4, 1)
    before_2 = jnp.where(upper, 2, 3)
    after_2 = jnp.where(upper, 3, 2)
    at = at + jnp.where(gap == -1, before_1, 0) + jnp.where(gap == 1, after_1, 0)
    at = at + jnp.where(gap == -2, before_2, 0) + jnp.where(gap == 2, after_2, 0)
    for level in range(2, levels):
        at = at + jnp.where(gap == -(1 << level), 1 + 2 * level, 0)
        at = at + jnp.where(gap == (1 << level), 2 + 2 * level, 0)
    return at


def chunk_count(heads):
    for n in (4, 2):
        if heads % n == 0:
            return n
    return 1


def local(queries, keys, values, policy_grad, ref_velocity, key_lists, frame_tokens):
    rows, cols = queries.shape
    heads = cols // HD
    blocks = rows // BLK
    list_len = key_lists.shape[1]
    levels = lax.axis_size("frame").bit_length() - 1
    all_features = cols * lax.axis_size("head")
    me = lax.axis_index("frame")
    corner_of = me % 4
    corner = (corner_of == 0) | (corner_of == 3)
    upper = corner_of >= 2
    where = (places(key_lists // blocks - me, me, levels) * blocks + key_lists % blocks).reshape(-1)
    ids = jnp.arange(frame_tokens.shape[0], dtype=jnp.int32)
    counts = jnp.sum(
        jnp.where(key_lists.reshape(-1, 1) == ids[None, :], frame_tokens[None, :], 0), axis=-1
    ).astype(jnp.int32)
    n_chunks = chunk_count(heads)
    each = heads // n_chunks
    wide = each * HD
    pools, forwards = [], []
    for c in range(n_chunks):
        cut = slice(c * wide, (c + 1) * wide)
        kv = jnp.concatenate([keys[:, cut], values[:, cut]], axis=0)
        pools.append(gather(kv, corner, upper, levels))
    for c in range(n_chunks):
        forwards.append(
            forward(
                where, counts, queries, ref_velocity, pools[c], c * each, each, blocks, list_len
            )
        )
    squares = sum(f[2] for f in forwards)
    kl = lax.psum(jnp.sum(squares, axis=-1), "head") / all_features
    inv = jnp.broadcast_to((1.0 / (1.0 + kl))[:, None], (rows, HD))
    grad_q, grad_k, grad_v = [], [], []
    for c in range(n_chunks):
        attn, probs, _ = forwards[c]
        dq, *parts = backward(
            where, queries, policy_grad, ref_velocity, attn, probs, inv,
            pools[c], c * each, each, blocks, list_len,
        )
        total = scatter(parts, corner, upper, levels)
        grad_q.append(dq)
        grad_k.append(total[:rows])
        grad_v.append(total[rows:])
    return tuple(jnp.concatenate(x, axis=1) for x in (grad_q, grad_k, grad_v))


def solution(mesh):
    cut = P("frame", "head")
    return jax.shard_map(
        local,
        mesh=mesh,
        in_specs=(cut,) * 5 + (P("frame", None), P()),
        out_specs=(cut,) * 3,
        check_vma=False,
    )
```

```python
import functools
import math

import jax
import jax.numpy as jnp
from jax import lax
from jax.experimental import pallas as pl
from jax.experimental.pallas import tpu as pltpu
from jax.sharding import PartitionSpec as P

HD = 128
BLK = 128
KL_WEIGHT = 1.0
VMEM = 40 * 1024 * 1024

NT = (((1,), (1,)), ((), ()))
NN = (((1,), (0,)), ((), ()))
TN = (((0,), (0,)), ((), ()))


def dot(a, b, dims):
    return lax.dot_general(a, b, dims, preferred_element_type=jnp.float32)


def fetch(pool, held, sems, head, slot):
    cols = pl.ds(pl.multiple_of(head * HD, HD), HD)
    return [
        pltpu.make_async_copy(ref.at[:, cols], held.at[slot, n], sems.at[slot, n])
        for n, ref in enumerate(pool)
    ]


def rotate_in(pool, held, sems, head, heads):
    slot = lax.rem(head, 2)

    @pl.when(head == 0)
    def _():
        for copy in fetch(pool, held, sems, head, slot):
            copy.start()

    @pl.when(head + 1 < heads)
    def _():
        for copy in fetch(pool, held, sems, head + 1, 1 - slot):
            copy.start()

    for copy in fetch(pool, held, sems, head, slot):
        copy.wait()
    return slot


def listed(held, slot, where_ref, first, list_len, rows, part):
    out = []
    for n in range(list_len):
        code = where_ref[first + n]
        start = pl.multiple_of(lax.rem(code, rows // BLK) * BLK + part * rows, BLK)
        out.append(held[slot, lax.div(code, rows // BLK), pl.ds(start, BLK), :])
    return jnp.concatenate(out, axis=0)


def forward_kernel(n_pool, blocks, list_len, heads, where_ref, count_ref, q_ref, ref_ref, *rest):
    pool, (attn_ref, probs_ref, sq_ref, held, sems) = rest[:n_pool], rest[n_pool:]
    head = pl.program_id(0)
    rows = blocks * BLK
    slot = rotate_in(pool, held, sems, head, heads)
    scale = 1.0 / math.sqrt(HD)
    lane = lax.broadcasted_iota(jnp.int32, (BLK, BLK), 1)

    @pl.when(head == 0)
    def _():
        sq_ref[...] = jnp.zeros_like(sq_ref)

    for b in range(blocks):
        mine = pl.ds(b * BLK, BLK)
        k = listed(held, slot, where_ref, b * list_len, list_len, rows, 0)
        v = listed(held, slot, where_ref, b * list_len, list_len, rows, 1)
        s = dot(q_ref[mine, :], k, NT) * scale
        s = jnp.concatenate(
            [
                jnp.where(
                    lane < count_ref[b * list_len + n], s[:, n * BLK : (n + 1) * BLK], -1e30
                )
                for n in range(list_len)
            ],
            axis=1,
        )
        e = jnp.exp(s - jnp.max(s, axis=-1, keepdims=True))
        p = e * (1.0 / jnp.sum(e, axis=-1, keepdims=True))
        p16 = p.astype(jnp.bfloat16)
        probs_ref[0, mine, :] = p16
        attn = dot(p16, v, NN)
        attn_ref[mine, :] = attn
        diff = attn - ref_ref[mine, :].astype(jnp.float32)
        sq_ref[mine, :] += diff * diff


def backward_kernel(
    n_pool, blocks, list_len, heads, where_ref, q_ref, pg_ref, ref_ref, attn_ref, probs_ref, inv_ref, *rest
):
    pool, dq_ref, outs = rest[:n_pool], rest[n_pool], rest[n_pool + 1 : 2 * n_pool + 1]
    held, sems, part, out_sems = rest[2 * n_pool + 1 :]
    head = pl.program_id(0)
    rows = blocks * BLK
    slot = rotate_in(pool, held, sems, head, heads)
    scale = 1.0 / math.sqrt(HD)

    def leave(which, at):
        cols = pl.ds(pl.multiple_of(which * HD, HD), HD)
        return [
            pltpu.make_async_copy(part.at[at, n], ref.at[:, cols], out_sems.at[at, n])
            for n, ref in enumerate(outs)
        ]

    @pl.when(head >= 2)
    def _():
        for copy in leave(head - 2, slot):
            copy.wait()

    part[slot] = jnp.zeros(part.shape[1:], part.dtype)
    for b in range(blocks):
        mine = pl.ds(b * BLK, BLK)
        k = listed(held, slot, where_ref, b * list_len, list_len, rows, 0)
        v = listed(held, slot, where_ref, b * list_len, list_len, rows, 1)
        attn = attn_ref[mine, :]
        q = q_ref[mine, :]
        p16 = probs_ref[0, mine, :]
        diff = attn - ref_ref[mine, :].astype(jnp.float32)
        g16 = (pg_ref[mine, :].astype(jnp.float32) + KL_WEIGHT * diff * inv_ref[mine, :]).astype(
            jnp.bfloat16
        )
        delta = jnp.sum(g16.astype(jnp.float32) * attn, axis=-1, keepdims=True)
        ds16 = (p16.astype(jnp.float32) * (dot(g16, v, NT) - delta)).astype(jnp.bfloat16)
        dq_ref[mine, :] = (dot(ds16, k, NN) * scale).astype(jnp.bfloat16)
        dk = dot(ds16, q, TN) * scale
        dv = dot(p16, g16, TN)
        for n in range(list_len):
            code = where_ref[b * list_len + n]
            at, within = lax.div(code, blocks), lax.rem(code, blocks)
            for kind, value in ((0, dk), (1, dv)):
                start = pl.multiple_of(within * BLK + kind * rows, BLK)
                piece = value[n * BLK : (n + 1) * BLK, :]
                if b > 0:
                    piece = piece + part[slot, at, pl.ds(start, BLK), :].astype(jnp.float32)
                part[slot, at, pl.ds(start, BLK), :] = piece.astype(jnp.bfloat16)

    for copy in leave(head, slot):
        copy.start()

    @pl.when(head == heads - 1)
    def _():
        if heads > 1:
            for copy in leave(head - 1, 1 - slot):
                copy.wait()
        for copy in leave(head, slot):
            copy.wait()


def forward(where, counts, queries, ref, pool, first, heads, blocks, list_len):
    rows, keys = blocks * BLK, list_len * BLK
    n_pool = len(pool)
    column = pl.BlockSpec((rows, HD), lambda h, *_: (0, first + h))
    here = pl.BlockSpec((rows, HD), lambda h, *_: (0, h))
    return pl.pallas_call(
        functools.partial(forward_kernel, n_pool, blocks, list_len, heads),
        grid_spec=pltpu.PrefetchScalarGridSpec(
            num_scalar_prefetch=2,
            grid=(heads,),
            in_specs=[column, column] + [pl.BlockSpec(memory_space=pl.ANY)] * n_pool,
            out_specs=[
                here,
                pl.BlockSpec((1, rows, keys), lambda h, *_: (h, 0, 0)),
                pl.BlockSpec((rows, HD), lambda h, *_: (0, 0)),
            ],
            scratch_shapes=[
                pltpu.VMEM((2, n_pool, 2 * rows, HD), jnp.bfloat16),
                pltpu.SemaphoreType.DMA((2, n_pool)),
            ],
        ),
        out_shape=[
            jax.ShapeDtypeStruct((rows, heads * HD), jnp.float32),
            jax.ShapeDtypeStruct((heads, rows, keys), jnp.bfloat16),
            jax.ShapeDtypeStruct((rows, HD), jnp.float32),
        ],
        compiler_params=pltpu.CompilerParams(vmem_limit_bytes=VMEM),
        cost_estimate=pl.CostEstimate(
            flops=4 * heads * rows * keys * HD,
            bytes_accessed=heads * (n_pool * 4 * rows * HD + rows * keys * 2 + rows * HD * 8),
            transcendentals=heads * rows * keys,
        ),
        name="forward",
    )(where, counts, queries, ref, *pool)


def backward(where, queries, policy, ref, attn, probs, inv, pool, first, heads, blocks, list_len):
    rows, keys = blocks * BLK, list_len * BLK
    n_pool = len(pool)
    column = pl.BlockSpec((rows, HD), lambda h, *_: (0, first + h))
    here = pl.BlockSpec((rows, HD), lambda h, *_: (0, h))
    anywhere = pl.BlockSpec(memory_space=pl.ANY)
    return pl.pallas_call(
        functools.partial(backward_kernel, n_pool, blocks, list_len, heads),
        grid_spec=pltpu.PrefetchScalarGridSpec(
            num_scalar_prefetch=1,
            grid=(heads,),
            in_specs=[
                column,
                column,
                column,
                here,
                pl.BlockSpec((1, rows, keys), lambda h, *_: (h, 0, 0)),
                pl.BlockSpec((rows, HD), lambda h, *_: (0, 0)),
            ]
            + [anywhere] * n_pool,
            out_specs=[here] + [anywhere] * n_pool,
            scratch_shapes=[
                pltpu.VMEM((2, n_pool, 2 * rows, HD), jnp.bfloat16),
                pltpu.SemaphoreType.DMA((2, n_pool)),
                pltpu.VMEM((2, n_pool, 2 * rows, HD), jnp.bfloat16),
                pltpu.SemaphoreType.DMA((2, n_pool)),
            ],
        ),
        out_shape=[jax.ShapeDtypeStruct((rows, heads * HD), jnp.bfloat16)]
        + [jax.ShapeDtypeStruct((2 * rows, heads * HD), jnp.bfloat16)] * n_pool,
        compiler_params=pltpu.CompilerParams(vmem_limit_bytes=VMEM),
        cost_estimate=pl.CostEstimate(
            flops=8 * heads * rows * keys * HD,
            bytes_accessed=heads * (n_pool * 8 * rows * HD + rows * keys * 2 + rows * HD * 12),
            transcendentals=0,
        ),
        name="backward",
    )(where, queries, policy, ref, attn, probs, inv, *pool)


MESH = pl.DeviceIdType.MESH
PIECE = 64
STRIP = 16


class Place:
    def __init__(self, count):
        me = lax.axis_index("frame")
        self.count = count
        self.me = me
        self.x = me + 1 - 2 * (me % 2)
        self.y = me + 2 - 4 * ((me // 2) % 2)
        at = me % 4
        self.corner = (at == 0) | (at == 3)
        self.inner = jnp.logical_not(self.corner)
        self.upper = at >= 2
        self.lower = at < 2
        low, high = me >= 4, me + 4 < count
        self.has_cross = (self.lower & low) | (self.upper & high)
        self.gives_cross = (self.upper & low) | (self.lower & high)


def mover(send, recv, rows_of):
    def move(src, dst, n, p, target):
        rows = rows_of(p)
        return pltpu.make_async_remote_copy(
            src_ref=src.at[rows],
            dst_ref=dst.at[rows],
            send_sem=send.at[n, p],
            recv_sem=recv.at[n, p],
            device_id={"frame": target},
            device_id_type=MESH,
        )

    return move


def rows_of(p):
    return pl.ds(pl.multiple_of(p * PIECE, PIECE), PIECE)


def both(a, b):
    return jnp.logical_and(a, b)


def gather_kernel(count, levels, pieces, kv, *rest):
    outs, (send, recv) = rest[:-2], rest[-2:]
    x, y, cross, diagonal = outs[:4]
    at = Place(count)
    me = at.me
    move = mover(send, recv, rows_of)

    def before(level):
        return 2 * level

    def after(level):
        return 2 * level + 1

    @pl.loop(0, pieces)
    def _(p):
        @pl.when(me + 4 < count)
        def _():
            move(kv, outs[4], 4, p, me + 4).start()

        @pl.when(me >= 4)
        def _():
            move(kv, outs[5], 5, p, me - 4).start()

        move(kv, y, 1, p, at.y).start()
        move(kv, x, 0, p, at.x).start()

    for level in range(2, levels):
        step = 1 << level
        b, a = before(level), after(level)

        @pl.loop(0, pieces)
        def _(p):
            @pl.when(me >= step)
            def _():
                move(kv, outs[b], b, p, at.x).wait_recv()
                if level + 1 < levels:

                    @pl.when(me + step < count)
                    def _():
                        move(outs[b], outs[b + 2], b + 2, p, me + step).start()

                if level == 2:

                    @pl.when(at.upper)
                    def _():
                        move(outs[b], cross, 2, p, at.y).start()

            @pl.when(me + step < count)
            def _():
                move(kv, outs[a], a, p, at.x).wait_recv()
                if level + 1 < levels:

                    @pl.when(me >= step)
                    def _():
                        move(outs[a], outs[a + 2], a + 2, p, me - step).start()

                if level == 2:

                    @pl.when(at.lower)
                    def _():
                        move(outs[a], cross, 2, p, at.y).start()

            if level == 2:
                move(kv, y, 1, p, at.x).wait_recv()

                @pl.when(at.corner)
                def _():
                    move(y, diagonal, 3, p, at.x).start()

        if level == 2:

            @pl.loop(0, pieces)
            def _(p):
                @pl.when(at.has_cross)
                def _():
                    move(kv, cross, 2, p, at.x).wait_recv()

                    @pl.when(at.inner)
                    def _():
                        move(cross, diagonal, 3, p, at.x).start()

    @pl.loop(0, pieces)
    def _(p):
        move(kv, x, 0, p, at.x).wait_recv()
        move(kv, x, 0, p, at.x).wait_send()
        move(kv, y, 1, p, at.x).wait_send()

        @pl.when(at.inner | at.has_cross)
        def _():
            move(kv, diagonal, 3, p, at.x).wait_recv()

        @pl.when(at.corner | at.has_cross)
        def _():
            move(kv, diagonal, 3, p, at.x).wait_send()

        @pl.when(at.gives_cross)
        def _():
            move(kv, cross, 2, p, at.x).wait_send()

        for level in range(2, levels):
            step = 1 << (level - 1) if level > 2 else 4
            start = step if level > 2 else 0
            b, a = before(level), after(level)

            @pl.when(both(me >= start, me + step < count))
            def _():
                move(kv, outs[b], b, p, at.x).wait_send()

            @pl.when(both(me + start < count, me >= step))
            def _():
                move(kv, outs[a], a, p, at.x).wait_send()


def scatter_kernel(count, levels, pieces, *refs):
    n = 2 * levels
    parts, out = refs[: n + 1], refs[n + 1]
    held, land, send, recv, local_sems, out_sems = refs[n + 2 :]
    own, parts = parts[0], parts[1:]
    at = Place(count)
    me = at.me
    move = mover(send, recv, rows_of)
    kept = [n, 1, 2] + list(range(4, n - 2))

    def bring(slot):
        return pltpu.make_async_copy(
            own if slot == n else parts[slot], held.at[slot], local_sems.at[slot]
        )

    def leave(p):
        return pltpu.make_async_copy(held.at[n, rows_of(p)], out.at[rows_of(p)], out_sems.at[p])

    def add_to(slot, others, p):
        for j in range(PIECE // STRIP):
            rows = pl.ds(pl.multiple_of(p * PIECE + j * STRIP, STRIP), STRIP)
            total = held[slot, rows, :].astype(jnp.float32)
            for other in others:
                total = total + land[other, rows, :].astype(jnp.float32)
            held[slot, rows, :] = total.astype(jnp.bfloat16)

    for slot in kept:
        bring(slot).start()

    top_b, top_a = n - 2, n - 1
    reach, hop = 1 << (levels - 1), 1 << (levels - 2)

    @pl.loop(0, pieces)
    def _(p):
        move(parts[3], land.at[3], 3, p, at.x).start()
        if levels > 3:

            @pl.when(me >= reach)
            def _():
                move(parts[top_b], land.at[top_b], top_b, p, me - hop).start()

            @pl.when(me + reach < count)
            def _():
                move(parts[top_a], land.at[top_a], top_a, p, me + hop).start()

    @pl.loop(0, pieces)
    def _(p):
        move(parts[0], land.at[0], 0, p, at.x).start()

    for slot in kept:
        bring(slot).wait()

    @pl.loop(0, pieces)
    def _(p):
        move(own, land.at[3], 3, p, at.x).wait_recv()

        @pl.when(at.corner)
        def _():
            add_to(1, [3], p)

        @pl.when(at.inner)
        def _():
            add_to(2, [3], p)

        move(held.at[2], land.at[2], 2, p, at.y).start()
        move(held.at[1], land.at[1], 1, p, at.y).start()

    for level in range(levels - 2, 1, -1):
        b, a = 2 * level, 2 * level + 1
        step = 1 << level
        back = 4 if level == 2 else step // 2

        @pl.loop(0, pieces)
        def _(p):
            @pl.when(both(me >= step, me + step < count))
            def _():
                move(own, land.at[b + 2], b + 2, p, at.x).wait_recv()
                add_to(b, [b + 2], p)

            @pl.when(both(me >= step, me + step < count))
            def _():
                move(own, land.at[a + 2], a + 2, p, at.x).wait_recv()
                add_to(a, [a + 2], p)

            if level == 2:
                move(own, land.at[2], 2, p, at.x).wait_recv()

                @pl.when(at.upper)
                def _():
                    add_to(4, [2], p)

                @pl.when(at.lower)
                def _():
                    add_to(5, [2], p)

            @pl.when(me >= step)
            def _():
                move(held.at[b], land.at[b], b, p, me - back).start()

            @pl.when(me + step < count)
            def _():
                move(held.at[a], land.at[a], a, p, me + back).start()

    @pl.loop(0, pieces)
    def _(p):
        move(own, land.at[0], 0, p, at.x).wait_recv()
        move(own, land.at[1], 1, p, at.x).wait_recv()
        add_to(n, [0, 1], p)

        @pl.when(me + 4 < count)
        def _():
            move(own, land.at[4], 4, p, at.x).wait_recv()
            add_to(n, [4], p)

        @pl.when(me >= 4)
        def _():
            move(own, land.at[5], 5, p, at.x).wait_recv()
            add_to(n, [5], p)

        leave(p).start()

    @pl.loop(0, pieces)
    def _(p):
        for slot in range(4):
            move(own, land.at[slot], slot, p, at.x).wait_send()
        for level in range(2, levels):
            b, a = 2 * level, 2 * level + 1

            @pl.when(me >= (1 << level))
            def _():
                move(own, land.at[b], b, p, at.x).wait_send()

            @pl.when(me + (1 << level) < count)
            def _():
                move(own, land.at[a], a, p, at.x).wait_send()

        leave(p).wait()


def gather(kv, levels):
    n, pieces = 2 * levels, kv.shape[0] // PIECE
    anywhere = pl.BlockSpec(memory_space=pl.ANY)
    return [kv] + list(
        pl.pallas_call(
            functools.partial(gather_kernel, lax.axis_size("frame"), levels, pieces),
            in_specs=[anywhere],
            out_specs=[anywhere] * n,
            out_shape=[jax.ShapeDtypeStruct(kv.shape, kv.dtype)] * n,
            scratch_shapes=[pltpu.SemaphoreType.DMA((n, pieces))] * 2,
            compiler_params=pltpu.CompilerParams(has_side_effects=True),
            name="gather",
        )(kv)
    )


def scatter(parts, levels):
    n, pieces = 2 * levels, parts[0].shape[0] // PIECE
    shape = parts[0].shape
    anywhere = pl.BlockSpec(memory_space=pl.ANY)
    return pl.pallas_call(
        functools.partial(scatter_kernel, lax.axis_size("frame"), levels, pieces),
        in_specs=[anywhere] * (n + 1),
        out_specs=anywhere,
        out_shape=jax.ShapeDtypeStruct(shape, jnp.bfloat16),
        scratch_shapes=[
            pltpu.VMEM((n + 1,) + shape, jnp.bfloat16),
            pltpu.VMEM((n,) + shape, jnp.bfloat16),
            pltpu.SemaphoreType.DMA((n, pieces)),
            pltpu.SemaphoreType.DMA((n, pieces)),
            pltpu.SemaphoreType.DMA((n + 1,)),
            pltpu.SemaphoreType.DMA((pieces,)),
        ],
        compiler_params=pltpu.CompilerParams(
            has_side_effects=True, vmem_limit_bytes=56 * 1024 * 1024
        ),
        name="scatter",
    )(*parts)


def places(gap, me, levels):
    corner_of = me % 4
    upper = corner_of >= 2
    odd = corner_of % 2 == 1
    at = jnp.zeros_like(gap)
    before_1 = jnp.where(odd, 1, 4)
    after_1 = jnp.where(odd, 4, 1)
    before_2 = jnp.where(upper, 2, 3)
    after_2 = jnp.where(upper, 3, 2)
    at = at + jnp.where(gap == -1, before_1, 0) + jnp.where(gap == 1, after_1, 0)
    at = at + jnp.where(gap == -2, before_2, 0) + jnp.where(gap == 2, after_2, 0)
    for level in range(2, levels):
        at = at + jnp.where(gap == -(1 << level), 1 + 2 * level, 0)
        at = at + jnp.where(gap == (1 << level), 2 + 2 * level, 0)
    return at


def local(queries, keys, values, policy_grad, ref_velocity, key_lists, frame_tokens):
    rows, cols = queries.shape
    heads = cols // HD
    blocks = rows // BLK
    list_len = key_lists.shape[1]
    levels = lax.axis_size("frame").bit_length() - 1
    all_features = cols * lax.axis_size("head")
    me = lax.axis_index("frame")
    where = (places(key_lists // blocks - me, me, levels) * blocks + key_lists % blocks).reshape(-1)
    ids = jnp.arange(frame_tokens.shape[0], dtype=jnp.int32)
    counts = jnp.sum(
        jnp.where(key_lists.reshape(-1, 1) == ids[None, :], frame_tokens[None, :], 0), axis=-1
    ).astype(jnp.int32)
    pool = gather(jnp.concatenate([keys, values], axis=0), levels)
    attn, probs, squares = forward(
        where, counts, queries, ref_velocity, pool, 0, heads, blocks, list_len
    )
    kl = lax.psum(jnp.sum(squares, axis=-1), "head") / all_features
    inv = jnp.broadcast_to((1.0 / (1.0 + kl))[:, None], (rows, HD))
    grad_q, *parts = backward(
        where, queries, policy_grad, ref_velocity, attn, probs, inv, pool, 0, heads, blocks, list_len
    )
    total = scatter(parts, levels)
    return grad_q, total[:rows], total[rows:]


def solution(mesh):
    cut = P("frame", "head")
    return jax.shard_map(
        local,
        mesh=mesh,
        in_specs=(cut,) * 5 + (P("frame", None), P()),
        out_specs=(cut,) * 3,
        check_vma=False,
    )
```

```python
import functools
import math

import jax
import jax.numpy as jnp
from jax import lax
from jax.experimental import pallas as pl
from jax.experimental.pallas import tpu as pltpu
from jax.sharding import PartitionSpec as P

HD = 128
BLK = 128
KL_WEIGHT = 1.0
VMEM = 60 * 1024 * 1024

NT = (((1,), (1,)), ((), ()))
NN = (((1,), (0,)), ((), ()))
TN = (((0,), (0,)), ((), ()))


def dot(a, b, dims):
    return lax.dot_general(a, b, dims, preferred_element_type=jnp.float32)


def fetch(pool, held, sems, head, slot):
    cols = pl.ds(pl.multiple_of(head * HD, HD), HD)
    return [
        pltpu.make_async_copy(ref.at[:, cols], held.at[slot, n], sems.at[slot, n])
        for n, ref in enumerate(pool)
    ]


def rotate_in(pool, held, sems, head, heads):
    slot = lax.rem(head, 2)

    @pl.when(head == 0)
    def _():
        for copy in fetch(pool, held, sems, head, slot):
            copy.start()

    @pl.when(head + 1 < heads)
    def _():
        for copy in fetch(pool, held, sems, head + 1, 1 - slot):
            copy.start()

    for copy in fetch(pool, held, sems, head, slot):
        copy.wait()
    return slot


def listed(held, slot, where_ref, first, list_len, rows, part):
    out = []
    for n in range(list_len):
        code = where_ref[first + n]
        start = pl.multiple_of(lax.rem(code, rows // BLK) * BLK + part * rows, BLK)
        out.append(held[slot, lax.div(code, rows // BLK), pl.ds(start, BLK), :])
    return jnp.concatenate(out, axis=0)


def forward_kernel(n_pool, blocks, list_len, heads, where_ref, count_ref, q_ref, ref_ref, *rest):
    pool, (attn_ref, probs_ref, sq_ref, held, sems) = rest[:n_pool], rest[n_pool:]
    head = pl.program_id(0)
    rows = blocks * BLK
    slot = rotate_in(pool, held, sems, head, heads)
    scale = 1.0 / math.sqrt(HD)
    lane = lax.broadcasted_iota(jnp.int32, (BLK, BLK), 1)

    @pl.when(head == 0)
    def _():
        sq_ref[...] = jnp.zeros_like(sq_ref)

    for b in range(blocks):
        mine = pl.ds(b * BLK, BLK)
        k = listed(held, slot, where_ref, b * list_len, list_len, rows, 0)
        v = listed(held, slot, where_ref, b * list_len, list_len, rows, 1)
        s = dot(q_ref[mine, :], k, NT) * scale
        s = jnp.concatenate(
            [
                jnp.where(
                    lane < count_ref[b * list_len + n], s[:, n * BLK : (n + 1) * BLK], -1e30
                )
                for n in range(list_len)
            ],
            axis=1,
        )
        e = jnp.exp(s - jnp.max(s, axis=-1, keepdims=True))
        p = e * (1.0 / jnp.sum(e, axis=-1, keepdims=True))
        p16 = p.astype(jnp.bfloat16)
        probs_ref[0, mine, :] = p16
        attn = dot(p16, v, NN)
        attn_ref[mine, :] = attn
        diff = attn - ref_ref[mine, :].astype(jnp.float32)
        sq_ref[mine, :] += diff * diff


def backward_kernel(
    n_pool, blocks, list_len, heads, where_ref, q_ref, pg_ref, ref_ref, attn_ref, probs_ref, inv_ref, *rest
):
    pool, dq_ref, outs = rest[:n_pool], rest[n_pool], rest[n_pool + 1 : 2 * n_pool + 1]
    held, sems, part, out_sems = rest[2 * n_pool + 1 :]
    head = pl.program_id(0)
    rows = blocks * BLK
    slot = rotate_in(pool, held, sems, head, heads)
    scale = 1.0 / math.sqrt(HD)

    def leave(which, at):
        cols = pl.ds(pl.multiple_of(which * HD, HD), HD)
        return [
            pltpu.make_async_copy(part.at[at, n], ref.at[:, cols], out_sems.at[at, n])
            for n, ref in enumerate(outs)
        ]

    @pl.when(head >= 2)
    def _():
        for copy in leave(head - 2, slot):
            copy.wait()

    part[slot] = jnp.zeros(part.shape[1:], part.dtype)
    for b in range(blocks):
        mine = pl.ds(b * BLK, BLK)
        k = listed(held, slot, where_ref, b * list_len, list_len, rows, 0)
        v = listed(held, slot, where_ref, b * list_len, list_len, rows, 1)
        attn = attn_ref[mine, :]
        q = q_ref[mine, :]
        p16 = probs_ref[0, mine, :]
        diff = attn - ref_ref[mine, :].astype(jnp.float32)
        g16 = (pg_ref[mine, :].astype(jnp.float32) + KL_WEIGHT * diff * inv_ref[mine, :]).astype(
            jnp.bfloat16
        )
        delta = jnp.sum(g16.astype(jnp.float32) * attn, axis=-1, keepdims=True)
        ds16 = (p16.astype(jnp.float32) * (dot(g16, v, NT) - delta)).astype(jnp.bfloat16)
        dq_ref[mine, :] = (dot(ds16, k, NN) * scale).astype(jnp.bfloat16)
        dk = dot(ds16, q, TN) * scale
        dv = dot(p16, g16, TN)
        for n in range(list_len):
            code = where_ref[b * list_len + n]
            at, within = lax.div(code, blocks), lax.rem(code, blocks)
            for kind, value in ((0, dk), (1, dv)):
                start = pl.multiple_of(within * BLK + kind * rows, BLK)
                piece = value[n * BLK : (n + 1) * BLK, :]
                if b > 0:
                    piece = piece + part[slot, at, pl.ds(start, BLK), :].astype(jnp.float32)
                part[slot, at, pl.ds(start, BLK), :] = piece.astype(jnp.bfloat16)

    for copy in leave(head, slot):
        copy.start()

    @pl.when(head == heads - 1)
    def _():
        if heads > 1:
            for copy in leave(head - 1, 1 - slot):
                copy.wait()
        for copy in leave(head, slot):
            copy.wait()


def forward(where, counts, queries, ref, pool, first, heads, blocks, list_len):
    rows, keys = blocks * BLK, list_len * BLK
    n_pool = len(pool)
    column = pl.BlockSpec((rows, HD), lambda h, *_: (0, first + h))
    here = pl.BlockSpec((rows, HD), lambda h, *_: (0, h))
    return pl.pallas_call(
        functools.partial(forward_kernel, n_pool, blocks, list_len, heads),
        grid_spec=pltpu.PrefetchScalarGridSpec(
            num_scalar_prefetch=2,
            grid=(heads,),
            in_specs=[column, column] + [pl.BlockSpec(memory_space=pl.ANY)] * n_pool,
            out_specs=[
                here,
                pl.BlockSpec((1, rows, keys), lambda h, *_: (h, 0, 0)),
                pl.BlockSpec((rows, HD), lambda h, *_: (0, 0)),
            ],
            scratch_shapes=[
                pltpu.VMEM((2, n_pool, 2 * rows, HD), jnp.bfloat16),
                pltpu.SemaphoreType.DMA((2, n_pool)),
            ],
        ),
        out_shape=[
            jax.ShapeDtypeStruct((rows, heads * HD), jnp.float32),
            jax.ShapeDtypeStruct((heads, rows, keys), jnp.bfloat16),
            jax.ShapeDtypeStruct((rows, HD), jnp.float32),
        ],
        compiler_params=pltpu.CompilerParams(vmem_limit_bytes=VMEM),
        cost_estimate=pl.CostEstimate(
            flops=4 * heads * rows * keys * HD,
            bytes_accessed=heads * (n_pool * 4 * rows * HD + rows * keys * 2 + rows * HD * 8),
            transcendentals=heads * rows * keys,
        ),
        name="forward",
    )(where, counts, queries, ref, *pool)


def backward(where, queries, policy, ref, attn, probs, inv, pool, first, heads, blocks, list_len):
    rows, keys = blocks * BLK, list_len * BLK
    n_pool = len(pool)
    column = pl.BlockSpec((rows, HD), lambda h, *_: (0, first + h))
    here = pl.BlockSpec((rows, HD), lambda h, *_: (0, h))
    anywhere = pl.BlockSpec(memory_space=pl.ANY)
    return pl.pallas_call(
        functools.partial(backward_kernel, n_pool, blocks, list_len, heads),
        grid_spec=pltpu.PrefetchScalarGridSpec(
            num_scalar_prefetch=1,
            grid=(heads,),
            in_specs=[
                column,
                column,
                column,
                here,
                pl.BlockSpec((1, rows, keys), lambda h, *_: (h, 0, 0)),
                pl.BlockSpec((rows, HD), lambda h, *_: (0, 0)),
            ]
            + [anywhere] * n_pool,
            out_specs=[here] + [anywhere] * n_pool,
            scratch_shapes=[
                pltpu.VMEM((2, n_pool, 2 * rows, HD), jnp.bfloat16),
                pltpu.SemaphoreType.DMA((2, n_pool)),
                pltpu.VMEM((2, n_pool, 2 * rows, HD), jnp.bfloat16),
                pltpu.SemaphoreType.DMA((2, n_pool)),
            ],
        ),
        out_shape=[jax.ShapeDtypeStruct((rows, heads * HD), jnp.bfloat16)]
        + [jax.ShapeDtypeStruct((2 * rows, heads * HD), jnp.bfloat16)] * n_pool,
        compiler_params=pltpu.CompilerParams(vmem_limit_bytes=VMEM),
        cost_estimate=pl.CostEstimate(
            flops=8 * heads * rows * keys * HD,
            bytes_accessed=heads * (n_pool * 8 * rows * HD + rows * keys * 2 + rows * HD * 12),
            transcendentals=0,
        ),
        name="backward",
    )(where, queries, policy, ref, attn, probs, inv, *pool)


MESH = pl.DeviceIdType.MESH
PIECE = 32
STRIP = 16


class Place:
    def __init__(self, count):
        me = lax.axis_index("frame")
        self.count = count
        self.me = me
        self.x = me + 1 - 2 * (me % 2)
        self.y = me + 2 - 4 * ((me // 2) % 2)
        at = me % 4
        self.corner = (at == 0) | (at == 3)
        self.inner = jnp.logical_not(self.corner)
        self.upper = at >= 2
        self.lower = at < 2
        low, high = me >= 4, me + 4 < count
        self.has_cross = (self.lower & low) | (self.upper & high)
        self.gives_cross = (self.upper & low) | (self.lower & high)


def mover(send, recv, rows_of):
    def move(src, dst, n, p, target):
        rows = rows_of(p)
        return pltpu.make_async_remote_copy(
            src_ref=src.at[rows],
            dst_ref=dst.at[rows],
            send_sem=send.at[n, p],
            recv_sem=recv.at[n, p],
            device_id={"frame": target},
            device_id_type=MESH,
        )

    return move


def rows_of(p):
    return pl.ds(pl.multiple_of(p * PIECE, PIECE), PIECE)


def both(a, b):
    return jnp.logical_and(a, b)


def gather_kernel(count, levels, pieces, kv, *rest):
    outs, (send, recv) = rest[:-2], rest[-2:]
    x, y, cross, diagonal = outs[:4]
    at = Place(count)
    me = at.me
    move = mover(send, recv, rows_of)

    def before(level):
        return 2 * level

    def after(level):
        return 2 * level + 1

    @pl.loop(0, pieces)
    def _(p):
        @pl.when(me + 4 < count)
        def _():
            move(kv, outs[4], 4, p, me + 4).start()

        @pl.when(me >= 4)
        def _():
            move(kv, outs[5], 5, p, me - 4).start()

        move(kv, y, 1, p, at.y).start()
        move(kv, x, 0, p, at.x).start()

    for level in range(2, levels):
        step = 1 << level
        b, a = before(level), after(level)

        @pl.loop(0, pieces)
        def _(p):
            @pl.when(me >= step)
            def _():
                move(kv, outs[b], b, p, at.x).wait_recv()
                if level + 1 < levels:

                    @pl.when(me + step < count)
                    def _():
                        move(outs[b], outs[b + 2], b + 2, p, me + step).start()

                if level == 2:

                    @pl.when(at.upper)
                    def _():
                        move(outs[b], cross, 2, p, at.y).start()

            @pl.when(me + step < count)
            def _():
                move(kv, outs[a], a, p, at.x).wait_recv()
                if level + 1 < levels:

                    @pl.when(me >= step)
                    def _():
                        move(outs[a], outs[a + 2], a + 2, p, me - step).start()

                if level == 2:

                    @pl.when(at.lower)
                    def _():
                        move(outs[a], cross, 2, p, at.y).start()

            if level == 2:
                move(kv, y, 1, p, at.x).wait_recv()

                @pl.when(at.corner)
                def _():
                    move(y, diagonal, 3, p, at.x).start()

        if level == 2:

            @pl.loop(0, pieces)
            def _(p):
                @pl.when(at.has_cross)
                def _():
                    move(kv, cross, 2, p, at.x).wait_recv()

                    @pl.when(at.inner)
                    def _():
                        move(cross, diagonal, 3, p, at.x).start()

    @pl.loop(0, pieces)
    def _(p):
        move(kv, x, 0, p, at.x).wait_recv()
        move(kv, x, 0, p, at.x).wait_send()
        move(kv, y, 1, p, at.x).wait_send()

        @pl.when(at.inner | at.has_cross)
        def _():
            move(kv, diagonal, 3, p, at.x).wait_recv()

        @pl.when(at.corner | at.has_cross)
        def _():
            move(kv, diagonal, 3, p, at.x).wait_send()

        @pl.when(at.gives_cross)
        def _():
            move(kv, cross, 2, p, at.x).wait_send()

        for level in range(2, levels):
            step = 1 << (level - 1) if level > 2 else 4
            start = step if level > 2 else 0
            b, a = before(level), after(level)

            @pl.when(both(me >= start, me + step < count))
            def _():
                move(kv, outs[b], b, p, at.x).wait_send()

            @pl.when(both(me + start < count, me >= step))
            def _():
                move(kv, outs[a], a, p, at.x).wait_send()


def scatter_kernel(count, levels, pieces, *refs):
    n = 2 * levels
    parts, out = refs[: n + 1], refs[n + 1]
    held, land, send, recv, local_sems, out_sems = refs[n + 2 :]
    own, parts = parts[0], parts[1:]
    at = Place(count)
    me = at.me
    move = mover(send, recv, rows_of)
    kept = [n, 1, 2] + list(range(4, n - 2))

    def bring(slot):
        return pltpu.make_async_copy(
            own if slot == n else parts[slot], held.at[slot], local_sems.at[slot]
        )

    def leave(p):
        return pltpu.make_async_copy(held.at[n, rows_of(p)], out.at[rows_of(p)], out_sems.at[p])

    def add_to(slot, others, p):
        for j in range(PIECE // STRIP):
            rows = pl.ds(pl.multiple_of(p * PIECE + j * STRIP, STRIP), STRIP)
            total = held[slot, rows, :].astype(jnp.float32)
            for other in others:
                total = total + land[other, rows, :].astype(jnp.float32)
            held[slot, rows, :] = total.astype(jnp.bfloat16)

    for slot in kept:
        bring(slot).start()

    top_b, top_a = n - 2, n - 1
    reach, hop = 1 << (levels - 1), 1 << (levels - 2)

    @pl.loop(0, pieces)
    def _(p):
        move(parts[3], land.at[3], 3, p, at.x).start()
        if levels > 3:

            @pl.when(me >= reach)
            def _():
                move(parts[top_b], land.at[top_b], top_b, p, me - hop).start()

            @pl.when(me + reach < count)
            def _():
                move(parts[top_a], land.at[top_a], top_a, p, me + hop).start()

    @pl.loop(0, pieces)
    def _(p):
        move(parts[0], land.at[0], 0, p, at.x).start()

    for slot in kept:
        bring(slot).wait()

    @pl.loop(0, pieces)
    def _(p):
        move(own, land.at[3], 3, p, at.x).wait_recv()

        @pl.when(at.corner)
        def _():
            add_to(1, [3], p)

        @pl.when(at.inner)
        def _():
            add_to(2, [3], p)

        move(held.at[2], land.at[2], 2, p, at.y).start()
        move(held.at[1], land.at[1], 1, p, at.y).start()

    for level in range(levels - 2, 1, -1):
        b, a = 2 * level, 2 * level + 1
        step = 1 << level
        back = 4 if level == 2 else step // 2

        @pl.loop(0, pieces)
        def _(p):
            @pl.when(both(me >= step, me + step < count))
            def _():
                move(own, land.at[b + 2], b + 2, p, at.x).wait_recv()
                add_to(b, [b + 2], p)

            @pl.when(both(me >= step, me + step < count))
            def _():
                move(own, land.at[a + 2], a + 2, p, at.x).wait_recv()
                add_to(a, [a + 2], p)

            if level == 2:
                move(own, land.at[2], 2, p, at.x).wait_recv()

                @pl.when(at.upper)
                def _():
                    add_to(4, [2], p)

                @pl.when(at.lower)
                def _():
                    add_to(5, [2], p)

            @pl.when(me >= step)
            def _():
                move(held.at[b], land.at[b], b, p, me - back).start()

            @pl.when(me + step < count)
            def _():
                move(held.at[a], land.at[a], a, p, me + back).start()

    @pl.loop(0, pieces)
    def _(p):
        move(own, land.at[0], 0, p, at.x).wait_recv()
        move(own, land.at[1], 1, p, at.x).wait_recv()
        add_to(n, [0, 1], p)

        @pl.when(me + 4 < count)
        def _():
            move(own, land.at[4], 4, p, at.x).wait_recv()
            add_to(n, [4], p)

        @pl.when(me >= 4)
        def _():
            move(own, land.at[5], 5, p, at.x).wait_recv()
            add_to(n, [5], p)

        leave(p).start()

    @pl.loop(0, pieces)
    def _(p):
        for slot in range(4):
            move(own, land.at[slot], slot, p, at.x).wait_send()
        for level in range(2, levels):
            b, a = 2 * level, 2 * level + 1

            @pl.when(me >= (1 << level))
            def _():
                move(own, land.at[b], b, p, at.x).wait_send()

            @pl.when(me + (1 << level) < count)
            def _():
                move(own, land.at[a], a, p, at.x).wait_send()

        leave(p).wait()


def gather(kv, levels):
    n, pieces = 2 * levels, kv.shape[0] // PIECE
    anywhere = pl.BlockSpec(memory_space=pl.ANY)
    return [kv] + list(
        pl.pallas_call(
            functools.partial(gather_kernel, lax.axis_size("frame"), levels, pieces),
            in_specs=[anywhere],
            out_specs=[anywhere] * n,
            out_shape=[jax.ShapeDtypeStruct(kv.shape, kv.dtype)] * n,
            scratch_shapes=[pltpu.SemaphoreType.DMA((n, pieces))] * 2,
            compiler_params=pltpu.CompilerParams(has_side_effects=True),
            name="gather",
        )(kv)
    )


def scatter(parts, levels):
    n, pieces = 2 * levels, parts[0].shape[0] // PIECE
    shape = parts[0].shape
    anywhere = pl.BlockSpec(memory_space=pl.ANY)
    return pl.pallas_call(
        functools.partial(scatter_kernel, lax.axis_size("frame"), levels, pieces),
        in_specs=[anywhere] * (n + 1),
        out_specs=anywhere,
        out_shape=jax.ShapeDtypeStruct(shape, jnp.bfloat16),
        scratch_shapes=[
            pltpu.VMEM((n + 1,) + shape, jnp.bfloat16),
            pltpu.VMEM((n,) + shape, jnp.bfloat16),
            pltpu.SemaphoreType.DMA((n, pieces)),
            pltpu.SemaphoreType.DMA((n, pieces)),
            pltpu.SemaphoreType.DMA((n + 1,)),
            pltpu.SemaphoreType.DMA((pieces,)),
        ],
        compiler_params=pltpu.CompilerParams(
            has_side_effects=True, vmem_limit_bytes=VMEM
        ),
        name="scatter",
    )(*parts)


def places(gap, me, levels):
    corner_of = me % 4
    upper = corner_of >= 2
    odd = corner_of % 2 == 1
    at = jnp.zeros_like(gap)
    before_1 = jnp.where(odd, 1, 4)
    after_1 = jnp.where(odd, 4, 1)
    before_2 = jnp.where(upper, 2, 3)
    after_2 = jnp.where(upper, 3, 2)
    at = at + jnp.where(gap == -1, before_1, 0) + jnp.where(gap == 1, after_1, 0)
    at = at + jnp.where(gap == -2, before_2, 0) + jnp.where(gap == 2, after_2, 0)
    for level in range(2, levels):
        at = at + jnp.where(gap == -(1 << level), 1 + 2 * level, 0)
        at = at + jnp.where(gap == (1 << level), 2 + 2 * level, 0)
    return at


def local(queries, keys, values, policy_grad, ref_velocity, key_lists, frame_tokens):
    rows, cols = queries.shape
    heads = cols // HD
    blocks = rows // BLK
    list_len = key_lists.shape[1]
    levels = lax.axis_size("frame").bit_length() - 1
    all_features = cols * lax.axis_size("head")
    me = lax.axis_index("frame")
    where = (places(key_lists // blocks - me, me, levels) * blocks + key_lists % blocks).reshape(-1)
    ids = jnp.arange(frame_tokens.shape[0], dtype=jnp.int32)
    counts = jnp.sum(
        jnp.where(key_lists.reshape(-1, 1) == ids[None, :], frame_tokens[None, :], 0), axis=-1
    ).astype(jnp.int32)
    pool = gather(jnp.concatenate([keys, values], axis=0), levels)
    attn, probs, squares = forward(
        where, counts, queries, ref_velocity, pool, 0, heads, blocks, list_len
    )
    kl = lax.psum(jnp.sum(squares, axis=-1), "head") / all_features
    inv = jnp.broadcast_to((1.0 / (1.0 + kl))[:, None], (rows, HD))
    grad_q, *parts = backward(
        where, queries, policy_grad, ref_velocity, attn, probs, inv, pool, 0, heads, blocks, list_len
    )
    total = scatter(parts, levels)
    return grad_q, total[:rows], total[rows:]


def solution(mesh):
    cut = P("frame", "head")
    return jax.shard_map(
        local,
        mesh=mesh,
        in_specs=(cut,) * 5 + (P("frame", None), P()),
        out_specs=(cut,) * 3,
        check_vma=False,
    )
```
